128 devices in a mesh: dp: 16 (over x, y), graph: 8 (over z, core).
Axes of the slice: x: 4, y: 4, z: 4, core: 2. Of those that a mesh axis runs over, the one named last changes fastest.
Arguments:
- atom_embed: bfloat16 [16, 1024, 1024], P('dp', 'graph'), may hold values from -6 to 6
- edge_embed: bfloat16 [16, 8192, 1024], P('dp', 'graph'), may hold values from -6 to 6
- source: int32 [16, 8192], P('dp', 'graph'), may hold values from 0 to 1023
- target: int32 [16, 8192], P('dp', 'graph'), may hold values from 0 to 1023
- trip_source: int32 [16, 16384], P('dp', 'graph'), may hold values from 0 to 1023
- trip_target: int32 [16, 16384], P('dp', 'graph'), may hold values from 0 to 1023
- trip_count: int32 [16, 8], P('dp', 'graph'), may hold values from 1024 to 2048, as said below
- basis_values: bfloat16 [16, 16384, 128], P('dp', 'graph'), may hold values from -6 to 6
- w_pair: bfloat16 [2048, 1024], replicated, may hold values from -0.125 to 0.125
- w_basis: bfloat16 [128, 1024], replicated, may hold values from -0.5 to 0.5
- w_out: bfloat16 [1024, 1024], replicated, may hold values from -0.1875 to 0.1875
- w_atom: bfloat16 [1024, 1024], replicated, may hold values from -0.1875 to 0.1875
- atom_cotan: bfloat16 [16, 1024, 1024], P('dp', 'graph'), may hold values from -6 to 6
- edge_cotan: bfloat16 [16, 8192, 1024], P('dp', 'graph'), may hold values from -6 to 6
Outputs:
- new_atoms: bfloat16 [16, 1024, 1024], P('dp', 'graph')
- new_edges: bfloat16 [16, 8192, 1024], P('dp', 'graph')
- grad_atoms: bfloat16 [16, 1024, 1024], P('dp', 'graph')
- grad_edges: bfloat16 [16, 8192, 1024], P('dp', 'graph')
- grad_pair: float32 [2048, 1024], P(('dp', 'graph'))
- grad_basis: float32 [128, 1024], P(('dp', 'graph'))
- grad_out: float32 [1024, 1024], P(('dp', 'graph'))
- grad_atom: float32 [1024, 1024], P(('dp', 'graph'))
The draws below stay inside these ranges and needn't reach their ends.
Inputs may be any that keep to these rules, and one draw needn't show every extreme that they name: `trip_count`: block 0 of batch 0 is full; live slots come first in each block.
All inputs are finite; a program needn't handle non-finite values.
Results may differ from the reference program's by a relative error of at most 0.025.
Values may be sent and summed in bfloat16 or wider, within the bound.
No kernel may reach another device: no remote copies, remote signals or barrier semaphores. Data moves between devices by JAX's collectives and lax.ppermute only.
A program may use at most 128 MiB of HBM per device.

```python
import jax
import jax.numpy as jnp
from jax import lax

D = 1024
BASIS = 128
EDGE_DEV = 1024
TRIP_DEV = 2048
BATCHES = 16
ATOMS = 1024
EDGES = 8192
TRIPS = 16384
N_GRAPH = 8


def draw_trip_count(key, part):
    key = jax.random.fold_in(key, 7)
    counts = jax.random.randint(key, (BATCHES, N_GRAPH), TRIP_DEV // 2, TRIP_DEV + 1, dtype=jnp.int32)
    return counts.at[0, 0].set(TRIP_DEV)


def touch_ends(result, key, least, largest):
    longest = result.shape.index(max(result.shape))
    spots = []
    for shift in (0, 1):
        where = [jax.random.randint(jax.random.fold_in(key, axis), (), 0, length) for axis, length in enumerate(result.shape)]
        where[longest] = (where[longest] + shift) % result.shape[longest]
        spots.append(tuple(where))
    return result.at[spots[0]].set(least).at[spots[1]].set(largest)


def level_of(key, extent, shards, low, largest):
    def one(position, blocks):
        draws = jax.random.uniform(jax.random.fold_in(jax.random.fold_in(key, 6), position), (blocks,), jnp.float32, low / len(shards), largest / len(shards))
        return jnp.repeat(jnp.exp(draws), extent[position] // blocks).reshape((-1,) + (1,) * (len(extent) - position - 1))

    factor_of = one(*shards[0])
    for cut in shards[1:]:
        factor_of = factor_of * one(*cut)
    return factor_of


def noise(own_key, extent, deviation, reach, shards=(), held_as=jnp.bfloat16):
    array = deviation * jax.random.normal(own_key, extent, jnp.float32)
    if shards:
        array = array * level_of(own_key, extent, shards, -0.22, 0.18)
    return jnp.clip(array, -reach, reach).astype(held_as)


def setup_inputs(seed: int = 0) -> dict:
    seeds = jax.random.split(jax.random.key(seed), 15)
    return {
        "atom_embed": noise(seeds[0], (BATCHES, ATOMS, D), 1.0, 6.0, ((0, 16), (1, 8))),
        "edge_embed": noise(seeds[1], (BATCHES, EDGES, D), 1.0, 6.0, ((0, 16), (1, 8))),
        "source": touch_ends(jax.random.randint(seeds[2], (BATCHES, EDGES), 0, ATOMS), jax.random.fold_in(seeds[2], 1), 0, ATOMS - 1).astype(jnp.int32),
        "target": touch_ends(jax.random.randint(seeds[3], (BATCHES, EDGES), 0, ATOMS), jax.random.fold_in(seeds[3], 1), 0, ATOMS - 1).astype(jnp.int32),
        "trip_source": touch_ends(jax.random.randint(seeds[4], (BATCHES, TRIPS), 0, EDGE_DEV), jax.random.fold_in(seeds[4], 1), 0, EDGE_DEV - 1).astype(jnp.int32),
        "trip_target": touch_ends(jax.random.randint(seeds[5], (BATCHES, TRIPS), 0, EDGE_DEV), jax.random.fold_in(seeds[5], 1), 0, EDGE_DEV - 1).astype(jnp.int32),
        "trip_count": draw_trip_count(jax.random.fold_in(seeds[14], 71), 0),
        "basis_values": noise(seeds[7], (BATCHES, TRIPS, BASIS), 1.0, 6.0, ((0, 16), (1, 8))),
        "w_pair": noise(seeds[8], (2 * D, D), (2 * D) ** -0.5, 0.125),
        "w_basis": noise(seeds[9], (BASIS, D), BASIS ** -0.5, 0.5),
        "w_out": noise(seeds[10], (D, D), D ** -0.5, 0.1875),
        "w_atom": noise(seeds[11], (D, D), D ** -0.5, 0.1875),
        "atom_cotan": noise(seeds[12], (BATCHES, ATOMS, D), 1.0, 6.0, ((0, 16), (1, 8))),
        "edge_cotan": noise(seeds[13], (BATCHES, EDGES, D), 1.0, 6.0, ((0, 16), (1, 8))),
    }


SCALE = 8.0 ** -0.5


def silu_slope(value):
    sigma = jax.nn.sigmoid(value)
    return sigma * (1.0 + value * (1.0 - sigma))


def one_batch(atom_embed, edge_embed, source, target, trip_source, trip_target, trip_count, basis_values, w_pair, w_basis, w_out, w_atom, atom_cotan, edge_cotan):
    highest = lax.Precision.HIGHEST
    f32 = jnp.float32
    offsets = (jnp.arange(N_GRAPH, dtype=jnp.int32) * EDGE_DEV)[:, None]
    trip_in = (trip_source.reshape(N_GRAPH, TRIP_DEV) + offsets).reshape(-1)
    trip_tgt = (trip_target.reshape(N_GRAPH, TRIP_DEV) + offsets).reshape(-1)
    live = (jnp.arange(TRIP_DEV, dtype=jnp.int32)[None, :] < trip_count[:, None]).reshape(-1)[:, None]
    pair_src = w_pair[:D]
    pair_dst = w_pair[D:]
    proj_src = jnp.dot(atom_embed, pair_src, preferred_element_type=f32)
    proj_dst = jnp.dot(atom_embed, pair_dst, preferred_element_type=f32)
    preact = jnp.take(proj_src, source, axis=0) + jnp.take(proj_dst, target, axis=0)
    activated = jax.nn.silu(preact).astype(jnp.bfloat16)
    filters = jnp.dot(basis_values, w_basis, preferred_element_type=f32)
    in_rows = jnp.take(activated, trip_in, axis=0).astype(f32)
    trip_msg = jnp.where(live, in_rows * filters, 0.0).astype(jnp.bfloat16)
    summed = jnp.zeros((EDGES, D), f32).at[trip_tgt].add(trip_msg.astype(f32)).astype(jnp.bfloat16)
    edge_new = (edge_embed.astype(f32) + jnp.dot(summed, w_out, preferred_element_type=f32)).astype(jnp.bfloat16)
    partial_atoms = jnp.zeros((ATOMS, D), f32).at[target].add(edge_new.astype(f32))
    atom_sum = (partial_atoms * SCALE).astype(jnp.bfloat16)
    zvalue = jnp.dot(atom_sum, w_atom, preferred_element_type=f32)
    atoms_new = (atom_embed.astype(f32) + jax.nn.silu(zvalue)).astype(jnp.bfloat16)
    d_zvalue = (atom_cotan.astype(f32) * silu_slope(zvalue)).astype(jnp.bfloat16)
    grad_atom_w = jnp.einsum("ad,af->df", atom_sum.astype(f32), d_zvalue.astype(f32), precision=highest)
    d_atomsum = jnp.einsum("af,df->ad", d_zvalue.astype(f32), w_atom.astype(f32), precision=highest).astype(jnp.bfloat16)
    d_edge = (edge_cotan.astype(f32) + SCALE * jnp.take(d_atomsum, target, axis=0).astype(f32)).astype(jnp.bfloat16)
    grad_out_w = jnp.einsum("ed,ef->df", summed.astype(f32), d_edge.astype(f32), precision=highest)
    d_summed = jnp.einsum("ef,df->ed", d_edge.astype(f32), w_out.astype(f32), precision=highest).astype(jnp.bfloat16)
    d_trip = jnp.where(live, jnp.take(d_summed, trip_tgt, axis=0).astype(f32), 0.0)
    d_filter = (d_trip * in_rows).astype(jnp.bfloat16)
    grad_basis_w = jnp.einsum("tb,td->bd", basis_values.astype(f32), d_filter.astype(f32), precision=highest)
    d_active = jnp.zeros((EDGES, D), f32).at[trip_in].add(d_trip * filters)
    d_preact = (d_active * silu_slope(preact)).astype(jnp.bfloat16).astype(f32)
    sum_src = jnp.zeros((ATOMS, D), f32).at[source].add(d_preact)
    sum_dst = jnp.zeros((ATOMS, D), f32).at[target].add(d_preact)
    atoms32 = atom_embed.astype(f32)
    grad_pair_w = jnp.concatenate([jnp.dot(atoms32.T, sum_src, precision=highest), jnp.dot(atoms32.T, sum_dst, precision=highest)], axis=0)
    atom_back = jnp.dot(sum_src, pair_src.astype(f32).T, precision=highest) + jnp.dot(sum_dst, pair_dst.astype(f32).T, precision=highest)
    grads_new = (atom_cotan.astype(f32) + atom_back).astype(jnp.bfloat16)
    return (atoms_new, edge_new, grads_new, d_edge), (grad_pair_w, grad_basis_w, grad_out_w, grad_atom_w)


def reference(atom_embed, edge_embed, source, target, trip_source, trip_target, trip_count, basis_values, w_pair, w_basis, w_out, w_atom, atom_cotan, edge_cotan):
    def step(carry, batch):
        outputs, grads = one_batch(batch[0], batch[1], batch[2], batch[3], batch[4], batch[5], batch[6], batch[7], w_pair, w_basis, w_out, w_atom, batch[8], batch[9])
        carry = tuple(c + g for c, g in zip(carry, grads))
        return carry, outputs

    start = (jnp.zeros((2 * D, D), jnp.float32), jnp.zeros((BASIS, D), jnp.float32), jnp.zeros((D, D), jnp.float32), jnp.zeros((D, D), jnp.float32))
    totals, outputs = lax.scan(step, start, (atom_embed, edge_embed, source, target, trip_source, trip_target, trip_count, basis_values, atom_cotan, edge_cotan))
    return (outputs[0], outputs[1], outputs[2], outputs[3], totals[0], totals[1], totals[2], totals[3])
```

```python
import jax
import jax.numpy as jnp
from jax import lax
from jax.experimental import pallas as pl
from jax.experimental.pallas import tpu as pltpu
from jax.sharding import PartitionSpec as P

SCALE = 8.0 ** (-0.5)
BF = jnp.bfloat16
F32 = jnp.float32
VMEM_BYTES = 60 * 1024 * 1024
COL = 256


def dot_nn(a, b):
    return lax.dot_general(a, b, (((1,), (0,)), ((), ())), preferred_element_type=F32)


def dot_nt(a, b):
    return lax.dot_general(a, b, (((1,), (1,)), ((), ())), preferred_element_type=F32)


def dot_tn(a, b):
    return lax.dot_general(a, b, (((0,), (0,)), ((), ())), preferred_element_type=F32)


def silu_slope(value):
    sigma = jax.nn.sigmoid(value)
    return sigma * (1.0 + value * (1.0 - sigma))


def fill_gather(ref, index, at=0):
    length, width = index.shape[1], 1024
    column = jnp.broadcast_to(index, (128, length)).T
    lane = lax.broadcasted_iota(jnp.int32, (length, 128), 1)
    for b in range(width // 128):
        hit = jnp.where(column == lane + b * 128, 1.0, 0.0).astype(BF)
        ref[:, at + b * 128 : at + (b + 1) * 128] = hit


def fill_scatter(ref, index):
    length, width = index.shape[1], 1024
    sub = lax.broadcasted_iota(jnp.int32, (128, length), 0)
    for b in range(width // 128):
        hit = jnp.where(sub + b * 128 == index, 1.0, 0.0).astype(BF)
        ref[b * 128 : (b + 1) * 128, :] = hit


def full(shape):
    return pl.BlockSpec(shape, lambda j: (0,) * len(shape))


def cols(rows, width=COL):
    return pl.BlockSpec((rows, width), lambda j: (0, j))


def call(body, grid, in_specs, out_specs, out_shape, scratch, flops, moved, name):
    return pl.pallas_call(
        body,
        grid=grid,
        in_specs=in_specs,
        out_specs=out_specs,
        out_shape=out_shape,
        scratch_shapes=scratch,
        compiler_params=pltpu.CompilerParams(vmem_limit_bytes=VMEM_BYTES),
        cost_estimate=pl.CostEstimate(flops=flops, bytes_accessed=moved, transcendentals=0),
        name=name,
    )


def edge_body(*refs):
    blocks = refs[:8]
    src, dst, tin, ttg, w_pair, basis, w_basis = refs[8:15]
    rows, in_rows, slope, summed = refs[15:19]
    atoms, one_hot, gather_in, scatter_tgt, msg = refs[19:]

    @pl.when(pl.program_id(0) == 0)
    def _():
        for b in range(8):
            atoms[b * 128 : (b + 1) * 128, :] = blocks[b][...]
        for part, index in enumerate((src, dst)):
            fill_gather(one_hot, index[...])
            rows[:, part * 1024 : (part + 1) * 1024] = dot_nn(one_hot[...], atoms[...]).astype(BF)
        fill_gather(gather_in, tin[...])
        fill_scatter(scatter_tgt, ttg[...])

    preact = dot_nn(rows[...], w_pair[...])
    sigma = jax.nn.sigmoid(preact)
    slope[...] = (sigma * (1.0 + preact * (1.0 - sigma))).astype(BF)
    activated = (preact * sigma).astype(BF)
    for t in range(4):
        part = slice(t * 512, (t + 1) * 512)
        found = dot_nn(gather_in[part, :], activated)
        in_rows[part, :] = found.astype(BF)
        msg[part, :] = (found * dot_nn(basis[part, :], w_basis[...])).astype(BF)
    summed[...] = dot_nn(scatter_tgt[...], msg[...]).astype(BF)


def edge_forward(blocks, src, dst, tin, ttg, w_pair, basis, w_basis):
    return call(
        edge_body,
        (1024 // COL,),
        [full((128, 1024))] * 8
        + [full((1, 1024))] * 2
        + [full((1, 2048))] * 2
        + [cols(2048), full((2048, 128)), cols(128)],
        [full((1024, 2048)), cols(2048), cols(1024), cols(1024)],
        [
            jax.ShapeDtypeStruct((1024, 2048), BF),
            jax.ShapeDtypeStruct((2048, 1024), BF),
            jax.ShapeDtypeStruct((1024, 1024), BF),
            jax.ShapeDtypeStruct((1024, 1024), BF),
        ],
        [
            pltpu.VMEM((1024, 1024), BF),
            pltpu.VMEM((1024, 1024), BF),
            pltpu.VMEM((2048, 1024), BF),
            pltpu.VMEM((1024, 2048), BF),
            pltpu.VMEM((2048, COL), BF),
        ],
        int(2.15e9 * 8.3),
        20 << 20,
        "edge_forward",
    )(*blocks, src, dst, tin, ttg, w_pair, basis, w_basis)


def message_body(edge, summed, w_out, dst, new_edges, partial, scatter_dst):
    @pl.when(pl.program_id(0) == 0)
    def _():
        fill_scatter(scatter_dst, dst[...])

    new = (edge[...].astype(F32) + dot_nn(summed[...], w_out[...])).astype(BF)
    new_edges[...] = new
    partial[...] = dot_nn(scatter_dst[...], new).astype(BF)


def message_sum(edge, summed, w_out, dst):
    return call(
        message_body,
        (1024 // COL,),
        [cols(1024), full((1024, 1024)), cols(1024), full((1, 1024))],
        [cols(1024), cols(1024)],
        [jax.ShapeDtypeStruct((1024, 1024), BF)] * 2,
        [pltpu.VMEM((1024, 1024), BF)],
        int(2.15e9 * 2),
        10 << 20,
        "message_sum",
    )(edge, summed, w_out, dst)


def atom_body(y0, y1, y2, y3, atoms, cotan, w_atom, atom_sum, new_atoms, d_z, d_sum):
    total = y0[...].astype(F32) + y1[...].astype(F32) + y2[...].astype(F32) + y3[...].astype(F32)
    held = (total * SCALE).astype(BF)
    atom_sum[...] = held
    z = dot_nn(held, w_atom[...])
    sigma = jax.nn.sigmoid(z)
    new_atoms[...] = (atoms[...].astype(F32) + z * sigma).astype(BF)
    dz = (cotan[...].astype(F32) * (sigma * (1.0 + z * (1.0 - sigma)))).astype(BF)
    d_z[...] = dz
    d_sum[...] = dot_nt(dz, w_atom[...]).astype(BF)


def atom_update(ys, atoms, cotan, w_atom):
    return call(
        atom_body,
        (1,),
        [full((128, 1024))] * 6 + [full((1024, 1024))],
        [full((128, 1024))] * 4,
        [jax.ShapeDtypeStruct((128, 1024), BF)] * 4,
        [],
        int(2.15e9 / 4),
        5 << 20,
        "atom_update",
    )(*ys, atoms, cotan, w_atom)


def back_edge_body(*refs):
    blocks = refs[:8]
    dst, cotan, summed, w_out = refs[8:12]
    d_edge, grad_out, d_summed = refs[12:15]
    found, gather_dst, total = refs[15:]
    step = pl.program_id(0)

    @pl.when(step == 0)
    def _():
        fill_gather(gather_dst, dst[...])

    for b in range(8):
        found[b * 128 : (b + 1) * 128, :] = blocks[b][...]
    back = (cotan[...].astype(F32) + SCALE * dot_nn(gather_dst[...], found[...])).astype(BF)
    d_edge[...] = back
    grad_out[...] = dot_tn(summed[...], back).astype(BF)
    part = dot_nt(back, w_out[...])

    @pl.when(step == 0)
    def _():
        total[...] = part

    @pl.when(step > 0)
    def _():
        total[...] += part

    @pl.when(step == pl.num_programs(0) - 1)
    def _():
        d_summed[...] = total[...].astype(BF)


def edge_backward(blocks, dst, cotan, summed, w_out):
    return call(
        back_edge_body,
        (1024 // COL,),
        [cols(128)] * 8 + [full((1, 1024)), cols(1024), full((1024, 1024)), cols(1024)],
        [cols(1024), cols(1024), full((1024, 1024))],
        [jax.ShapeDtypeStruct((1024, 1024), BF)] * 3,
        [
            pltpu.VMEM((1024, COL), BF),
            pltpu.VMEM((1024, 1024), BF),
            pltpu.VMEM((1024, 1024), F32),
        ],
        int(2.15e9 * 3),
        14 << 20,
        "edge_backward",
    )(*blocks, dst, cotan, summed, w_out)


def trip_body(*refs):
    d_summed, in_rows, slope, basis, w_basis, rows, tin, ttg = refs[:8]
    grad_basis, d_preact, grad_pair = refs[8:11]
    gather_tgt, scatter_in, msg, d_filter = refs[11:]

    @pl.when(pl.program_id(0) == 0)
    def _():
        fill_gather(gather_tgt, ttg[...])
        fill_scatter(scatter_in, tin[...])

    for t in range(4):
        part = slice(t * 512, (t + 1) * 512)
        d_trip = dot_nn(gather_tgt[part, :], d_summed[...])
        d_filter[part, :] = (d_trip * in_rows[part, :].astype(F32)).astype(BF)
        msg[part, :] = (d_trip * dot_nn(basis[part, :], w_basis[...])).astype(BF)
    grad_basis[...] = dot_tn(basis[...], d_filter[...]).astype(BF)
    d_active = dot_nn(scatter_in[...], msg[...])
    d_pre = (d_active * slope[...].astype(F32)).astype(BF)
    d_preact[...] = d_pre
    grad_pair[...] = dot_tn(rows[...], d_pre).astype(BF)


def trip_backward(d_summed, in_rows, slope, basis, w_basis, rows, tin, ttg):
    return call(
        trip_body,
        (1024 // COL,),
        [
            cols(1024),
            cols(2048),
            cols(1024),
            full((2048, 128)),
            cols(128),
            full((1024, 2048)),
            full((1, 2048)),
            full((1, 2048)),
        ],
        [cols(128), cols(1024), cols(2048)],
        [
            jax.ShapeDtypeStruct((128, 1024), BF),
            jax.ShapeDtypeStruct((1024, 1024), BF),
            jax.ShapeDtypeStruct((2048, 1024), BF),
        ],
        [
            pltpu.VMEM((2048, 1024), BF),
            pltpu.VMEM((1024, 2048), BF),
            pltpu.VMEM((2048, COL), BF),
            pltpu.VMEM((2048, COL), BF),
        ],
        int(2.15e9 * 6.8),
        20 << 20,
        "trip_backward",
    )(d_summed, in_rows, slope, basis, w_basis, rows, tin, ttg)


def back_atom_body(d_preact, w_pair, src, dst, partial, scatter_src, scatter_dst, total):
    step = pl.program_id(0)

    @pl.when(step == 0)
    def _():
        fill_scatter(scatter_src, src[...])
        fill_scatter(scatter_dst, dst[...])

    held = d_preact[...]
    sum_src = dot_nn(scatter_src[...], held).astype(BF)
    sum_dst = dot_nn(scatter_dst[...], held).astype(BF)
    part = dot_nt(sum_src, w_pair[:1024, :]) + dot_nt(sum_dst, w_pair[1024:, :])

    @pl.when(step == 0)
    def _():
        total[...] = part

    @pl.when(step > 0)
    def _():
        total[...] += part

    @pl.when(step == pl.num_programs(0) - 1)
    def _():
        partial[...] = total[...].astype(BF)


def atom_backward(d_preact, w_pair, src, dst):
    return call(
        back_atom_body,
        (1024 // COL,),
        [cols(1024), cols(2048), full((1, 1024)), full((1, 1024))],
        full((1024, 1024)),
        jax.ShapeDtypeStruct((1024, 1024), BF),
        [
            pltpu.VMEM((1024, 1024), BF),
            pltpu.VMEM((1024, 1024), BF),
            pltpu.VMEM((1024, 1024), F32),
        ],
        int(2.15e9 * 4),
        10 << 20,
        "atom_backward",
    )(d_preact, w_pair, src, dst)


def grad_atom_body(atom_sum, d_z, out):
    out[...] = dot_tn(atom_sum[...], d_z[...]).astype(BF)


def atom_gradient(atom_sum, d_z):
    return call(
        grad_atom_body,
        (1,),
        [full((128, 1024))] * 2,
        full((1024, 1024)),
        jax.ShapeDtypeStruct((1024, 1024), BF),
        [],
        int(2.15e9 / 8),
        3 << 20,
        "atom_gradient",
    )(atom_sum, d_z)


def swap_core(x):
    return lax.ppermute(x, "graph", [(i, i ^ 1) for i in range(8)])


def along_z(x, shift):
    return lax.ppermute(
        x, "graph", [(2 * z + c, 2 * ((z + shift) % 4) + c) for z in range(4) for c in range(2)]
    )


def gather_graph(x):
    same = [x] + [along_z(x, -k) for k in (1, 2, 3)]
    return same + [swap_core(block) for block in same]


def scatter_graph(partial):
    size = partial.shape[0] // 2
    got = swap_core(partial[size:])
    both = (partial[:size].astype(F32) + got.astype(F32)).astype(BF).reshape(4, size // 4, -1)
    return [both[0]] + [along_z(both[k], k) for k in (1, 2, 3)]


def reduce_weights(grads, core):
    depths = [g.shape[0] // 128 for g in grads]
    joined = jnp.concatenate([g.reshape(16, 4, 2, d, 1024) for g, d in zip(grads, depths)], axis=3)
    keep = lax.dynamic_index_in_dim(joined, core, 2, keepdims=False)
    give = lax.dynamic_index_in_dim(joined, 1 - core, 2, keepdims=False)
    both = (keep.astype(F32) + swap_core(give).astype(F32)).astype(BF)
    spread = lax.all_to_all(both, "dp", 0, 0, tiled=True)
    plane = jnp.sum(spread.astype(F32), axis=0).astype(BF)
    last = lax.all_to_all(
        plane, "graph", 0, 0, tiled=True, axis_index_groups=[[0, 2, 4, 6], [1, 3, 5, 7]]
    )
    total = jnp.sum(last.astype(F32), axis=0)
    outs, at = [], 0
    for d in depths:
        outs.append(total[at : at + d])
        at += d
    return outs


def on_device(
    atom_embed,
    edge_embed,
    source,
    target,
    trip_source,
    trip_target,
    trip_count,
    basis_values,
    w_pair,
    w_basis,
    w_out,
    w_atom,
    atom_cotan,
    edge_cotan,
):
    place = lax.axis_index("graph")
    chip, core = place // 2, place % 2

    def local(index):
        owner = index // 128
        step = (owner // 2 - chip) & 3
        return (((owner & 1) ^ core) * 4 + step) * 128 + (index & 127)

    own_atoms, cotan = atom_embed[0], atom_cotan[0]
    src, dst = local(source), local(target)
    slot = lax.broadcasted_iota(jnp.int32, trip_target.shape, 1)
    tin, ttg = trip_source, jnp.where(slot < trip_count, trip_target, -1)
    basis = basis_values[0]

    blocks = gather_graph(own_atoms)
    rows, in_rows, slope, summed = edge_forward(blocks, src, dst, tin, ttg, w_pair, basis, w_basis)
    new_edges, partial = message_sum(edge_embed[0], summed, w_out, dst)
    atom_sum, new_atoms, d_z, d_sum = atom_update(scatter_graph(partial), own_atoms, cotan, w_atom)
    d_blocks = gather_graph(d_sum)
    grad_atom = atom_gradient(atom_sum, d_z)
    d_edge, grad_out, d_summed = edge_backward(d_blocks, dst, edge_cotan[0], summed, w_out)
    out_total, atom_w_total = reduce_weights([grad_out, grad_atom], core)
    grad_basis, d_preact, grad_pair = trip_backward(
        d_summed, in_rows, slope, basis, w_basis, rows, tin, ttg
    )
    back = scatter_graph(atom_backward(d_preact, w_pair, src, dst))
    grads_new = (cotan.astype(F32) + sum(b.astype(F32) for b in back)).astype(BF)
    pair_total, basis_total = reduce_weights([grad_pair, grad_basis], core)
    return (
        new_atoms[None],
        new_edges[None],
        grads_new[None],
        d_edge[None],
        pair_total,
        basis_total,
        out_total,
        atom_w_total,
    )


def solution(mesh):
    rows, flat = P("dp", "graph", None), P("dp", "graph")
    placed = (rows, rows, flat, flat, flat, flat, flat, rows, P(), P(), P(), P(), rows, rows)
    spread = P(("dp", "graph"), None)
    return jax.shard_map(
        on_device,
        mesh=mesh,
        in_specs=placed,
        out_specs=(rows,) * 4 + (spread,) * 4,
        check_vma=False,
    )
```

```python
import jax
import jax.numpy as jnp
from jax import lax
from jax.experimental import pallas as pl
from jax.experimental.pallas import tpu as pltpu
from jax.sharding import PartitionSpec as P

SCALE = 8.0 ** (-0.5)
BF = jnp.bfloat16
F32 = jnp.float32
COL = 512


def dot_nn(a, b):
    return lax.dot_general(a, b, (((1,), (0,)), ((), ())), preferred_element_type=F32)


def dot_nt(a, b):
    return lax.dot_general(a, b, (((1,), (1,)), ((), ())), preferred_element_type=F32)


def dot_tn(a, b):
    return lax.dot_general(a, b, (((0,), (0,)), ((), ())), preferred_element_type=F32)


def silu_slope(value):
    sigma = jax.nn.sigmoid(value)
    return sigma * (1.0 + value * (1.0 - sigma))


def fill_gather(ref, index, at=0):
    length, width = index.shape[1], 1024
    column = jnp.broadcast_to(index, (128, length)).T
    lane = lax.broadcasted_iota(jnp.int32, (length, 128), 1)
    for b in range(width // 128):
        hit = jnp.where(column == lane + b * 128, 1.0, 0.0).astype(BF)
        ref[:, at + b * 128 : at + (b + 1) * 128] = hit


def fill_scatter(ref, index):
    length, width = index.shape[1], 1024
    sub = lax.broadcasted_iota(jnp.int32, (128, length), 0)
    for b in range(width // 128):
        hit = jnp.where(sub + b * 128 == index, 1.0, 0.0).astype(BF)
        ref[b * 128 : (b + 1) * 128, :] = hit


def full(shape):
    return pl.BlockSpec(shape, lambda j: (0,) * len(shape))


def cols(rows, width=COL):
    return pl.BlockSpec((rows, width), lambda j: (0, j))


def call(body, grid, in_specs, out_specs, out_shape, scratch, flops, moved, mib, name):
    return pl.pallas_call(
        body,
        grid=grid,
        in_specs=in_specs,
        out_specs=out_specs,
        out_shape=out_shape,
        scratch_shapes=scratch,
        compiler_params=pltpu.CompilerParams(vmem_limit_bytes=mib << 20),
        cost_estimate=pl.CostEstimate(flops=flops, bytes_accessed=moved, transcendentals=0),
        name=name,
    )


STEPS = 1024 // COL


def early(rows, width=COL):
    return pl.BlockSpec((rows, width), lambda j: (0, jnp.minimum(j, STEPS - 1)))


def late(rows, width=COL):
    return pl.BlockSpec((rows, width), lambda j: (0, jnp.maximum(j - STEPS, 0)))


def prepare_body(basis, w_basis, filters, turned):
    filters[...] = dot_nn(basis[...], w_basis[...]).astype(BF)

    @pl.when(pl.program_id(0) == 0)
    def _():
        turned[...] = basis[...].T


def prepare(basis, w_basis):
    return call(
        prepare_body,
        (STEPS,),
        [full((2048, 128)), cols(128)],
        [cols(2048), full((128, 2048))],
        [jax.ShapeDtypeStruct((2048, 1024), BF), jax.ShapeDtypeStruct((128, 2048), BF)],
        [],
        int(2.15e9 * 0.6),
        6 << 20,
        60,
        "prepare",
    )(basis, w_basis)


def forward_body(*refs):
    blocks = refs[:8]
    src, dst, tin, ttg, w_pair, filters, edge, w_out = refs[8:16]
    rows_out, in_rows, slope, summed_out, new_edges, keep, give = refs[16:23]
    atoms, one_hot, gather_in, scatter_tgt, msg, rows, summed, sems = refs[23:]
    rows_copy = pltpu.make_async_copy(rows, rows_out, sems.at[0])
    summed_copy = pltpu.make_async_copy(summed, summed_out, sems.at[1])
    step = pl.program_id(0)

    @pl.when(step == 0)
    def _():
        for b in range(8):
            atoms[b * 128 : (b + 1) * 128, :] = blocks[b][...]
        for part, index in enumerate((src, dst)):
            fill_gather(one_hot, index[...])
            rows[:, part * 1024 : (part + 1) * 1024] = dot_nn(one_hot[...], atoms[...]).astype(BF)
        rows_copy.start()
        fill_gather(gather_in, tin[...])
        fill_scatter(scatter_tgt, ttg[...])

    @pl.when(step < STEPS)
    def _():
        preact = dot_nn(rows[...], w_pair[...])
        sigma = jax.nn.sigmoid(preact)
        slope[...] = (sigma * (1.0 + preact * (1.0 - sigma))).astype(BF)
        activated = (preact * sigma).astype(BF)
        for t in range(2):
            part = slice(t * 1024, (t + 1) * 1024)
            found = dot_nn(gather_in[part, :], activated).astype(BF)
            in_rows[part, :] = found
            msg[part, :] = found * filters[part, :]
        at = pl.ds(pl.multiple_of(step * COL, COL), COL)
        summed[:, at] = dot_nn(scatter_tgt[...], msg[...]).astype(BF)

    @pl.when(step == STEPS)
    def _():
        summed_copy.start()
        fill_scatter(one_hot, dst[...])

    @pl.when(step >= STEPS)
    def _():
        new = (edge[...].astype(F32) + dot_nn(summed[...], w_out[...])).astype(BF)
        new_edges[...] = new
        total = dot_nn(one_hot[...], new).astype(BF)
        keep[...] = total[:512]
        give[...] = total[512:]

    @pl.when(step == 2 * STEPS - 1)
    def _():
        rows_copy.wait()
        summed_copy.wait()


def forward(blocks, src, dst, tin, ttg, w_pair, filters, edge, w_out):
    return call(
        forward_body,
        (2 * STEPS,),
        [full((128, 1024))] * 8
        + [full((1, 1024))] * 2
        + [full((1, 2048))] * 2
        + [early(2048), early(2048), late(1024), late(1024)],
        [pl.BlockSpec(memory_space=pl.ANY), early(2048), early(1024), pl.BlockSpec(memory_space=pl.ANY)]
        + [late(1024), late(512), late(512)],
        [
            jax.ShapeDtypeStruct((1024, 2048), BF),
            jax.ShapeDtypeStruct((2048, 1024), BF),
            jax.ShapeDtypeStruct((1024, 1024), BF),
            jax.ShapeDtypeStruct((1024, 1024), BF),
            jax.ShapeDtypeStruct((1024, 1024), BF),
            jax.ShapeDtypeStruct((512, 1024), BF),
            jax.ShapeDtypeStruct((512, 1024), BF),
        ],
        [
            pltpu.VMEM((1024, 1024), BF),
            pltpu.VMEM((1024, 1024), BF),
            pltpu.VMEM((2048, 1024), BF),
            pltpu.VMEM((1024, 2048), BF),
            pltpu.VMEM((2048, COL), BF),
            pltpu.VMEM((1024, 2048), BF),
            pltpu.VMEM((1024, 1024), BF),
            pltpu.SemaphoreType.DMA((2,)),
        ],
        int(2.15e9 * 10.3),
        28 << 20,
        60,
        "forward",
    )(*blocks, src, dst, tin, ttg, w_pair, filters, edge, w_out)


def atom_body(y0, y1, y2, y3, atoms, cotan, w_atom, atom_sum, new_atoms, d_z, d_sum):
    total = y0[...].astype(F32) + y1[...].astype(F32) + y2[...].astype(F32) + y3[...].astype(F32)
    held = (total * SCALE).astype(BF)
    atom_sum[...] = held
    z = dot_nn(held, w_atom[...])
    sigma = jax.nn.sigmoid(z)
    new_atoms[...] = (atoms[...].astype(F32) + z * sigma).astype(BF)
    dz = (cotan[...].astype(F32) * (sigma * (1.0 + z * (1.0 - sigma)))).astype(BF)
    d_z[...] = dz
    d_sum[...] = dot_nt(dz, w_atom[...]).astype(BF)


def atom_update(ys, atoms, cotan, w_atom):
    return call(
        atom_body,
        (1,),
        [full((128, 1024))] * 6 + [full((1024, 1024))],
        [full((128, 1024))] * 4,
        [jax.ShapeDtypeStruct((128, 1024), BF)] * 4,
        [],
        int(2.15e9 / 4),
        5 << 20,
        14,
        "atom_update",
    )(*ys, atoms, cotan, w_atom)


def own_rows(core, even, odd, keep, give):
    even, odd = even.astype(BF), odd.astype(BF)
    keep[...] = jnp.where(core == 0, even, odd)
    give[...] = jnp.where(core == 0, odd, even)


SCALAR = pl.BlockSpec(memory_space=pltpu.SMEM)


def back_edge_body(*refs):
    blocks = refs[:8]
    core, dst, cotan, summed, atom_sum, d_z = refs[8:14]
    d_edge, keep, give = refs[14:17]
    found, gather_dst = refs[17:]

    @pl.when(pl.program_id(0) == 0)
    def _():
        fill_gather(gather_dst, dst[...])

    for b in range(8):
        found[b * 128 : (b + 1) * 128, :] = blocks[b][...]
    back = (cotan[...].astype(F32) + SCALE * dot_nn(gather_dst[...], found[...])).astype(BF)
    d_edge[...] = back
    out = dot_tn(summed[...], back).reshape(64, 2, 8, COL)
    atom = dot_tn(atom_sum[...], d_z[...]).reshape(64, 2, 8, COL)
    both = jnp.concatenate([out, atom], axis=2)
    own_rows(core[0], both[:, 0], both[:, 1], keep, give)


def edge_backward(blocks, core, dst, cotan, summed, atom_sum, d_z):
    chunks = pl.BlockSpec((64, 16, COL), lambda j: (0, 0, j))
    return call(
        back_edge_body,
        (STEPS,),
        [cols(128)] * 8
        + [SCALAR, full((1, 1024)), cols(1024), full((1024, 1024))]
        + [full((128, 1024)), cols(128)],
        [cols(1024), chunks, chunks],
        [
            jax.ShapeDtypeStruct((1024, 1024), BF),
            jax.ShapeDtypeStruct((64, 16, 1024), BF),
            jax.ShapeDtypeStruct((64, 16, 1024), BF),
        ],
        [pltpu.VMEM((1024, COL), BF), pltpu.VMEM((1024, 1024), BF)],
        int(2.15e9 * 2.2),
        12 << 20,
        40,
        "edge_backward",
    )(*blocks, core, dst, cotan, summed, atom_sum, d_z)


CHUNK = 1024 + 128
FOLD = 1024 // STEPS


def trip_body(*refs):
    core, d_summed, in_rows, slope, turned, filters, rows, tin, ttg = refs[:9]
    d_preact, keep, give = refs[9:12]
    gather_tgt, scatter_in, msg, d_filter, held, grad_basis, folded = refs[12:]
    step = pl.program_id(0)

    @pl.when(step == 0)
    def _():
        fill_gather(gather_tgt, ttg[...])
        fill_scatter(scatter_in, tin[...])

    @pl.when(step < STEPS)
    def _():
        for t in range(2):
            part = slice(t * 1024, (t + 1) * 1024)
            d_trip = dot_nn(gather_tgt[part, :], d_summed[...]).astype(BF)
            d_filter[part, :] = d_trip * in_rows[part, :]
            msg[part, :] = d_trip * filters[part, :]
        at = pl.ds(pl.multiple_of(step * COL, COL), COL)
        grad_basis[:, at] = dot_nn(turned[...], d_filter[...])
        d_active = dot_nn(scatter_in[...], msg[...])
        d_pre = (d_active * slope[...].astype(F32)).astype(BF)
        d_preact[...] = d_pre
        held[:, at] = d_pre

    @pl.when(step == STEPS)
    def _():
        for i in range(8):
            folded[pl.ds(i, 128, stride=8), :] = grad_basis[:, i * 128 : (i + 1) * 128]

    @pl.when(step >= STEPS)
    def _():
        both = dot_tn(rows[...], held[...]).reshape(64 // STEPS, 2, 16, 1024)
        at = pl.ds(pl.multiple_of((step - STEPS) * FOLD, FOLD), FOLD)
        fold = folded[at, :].reshape(64 // STEPS, 2, 8, 128)
        fold = jnp.concatenate([fold, jnp.zeros_like(fold)], axis=2)
        both = jnp.concatenate([both, fold], axis=3)
        own_rows(core[0], both[:, 0], both[:, 1], keep, give)


def own_rows(core, even, odd, keep, give):
    even, odd = even.astype(BF), odd.astype(BF)
    keep[...] = jnp.where(core == 0, even, odd)
    give[...] = jnp.where(core == 0, odd, even)


def trip_backward(core, d_summed, in_rows, slope, turned, filters, rows, tin, ttg):
    chunks = pl.BlockSpec((64 // STEPS, 16, CHUNK), lambda j: (jnp.maximum(j - STEPS, 0), 0, 0))
    return call(
        trip_body,
        (2 * STEPS,),
        [
            SCALAR,
            early(1024),
            early(2048),
            early(1024),
            full((128, 2048)),
            early(2048),
            late(1024, 2048 // STEPS),
            full((1, 2048)),
            full((1, 2048)),
        ],
        [early(1024), chunks, chunks],
        [
            jax.ShapeDtypeStruct((1024, 1024), BF),
            jax.ShapeDtypeStruct((64, 16, CHUNK), BF),
            jax.ShapeDtypeStruct((64, 16, CHUNK), BF),
        ],
        [
            pltpu.VMEM((2048, 1024), BF),
            pltpu.VMEM((1024, 2048), BF),
            pltpu.VMEM((2048, COL), BF),
            pltpu.VMEM((2048, COL), BF),
            pltpu.VMEM((1024, 1024), BF),
            pltpu.VMEM((128, 1024), F32),
            pltpu.VMEM((1024, 128), F32),
        ],
        int(2.15e9 * 6.6),
        24 << 20,
        60,
        "trip_backward",
    )(core, d_summed, in_rows, slope, turned, filters, rows, tin, ttg)


def project_body(d_edge, w_out, d_summed):
    d_summed[...] = dot_nt(d_edge[...], w_out[...]).astype(BF)


def project_back(d_edge, w_out):
    return call(
        project_body,
        (STEPS,),
        [full((1024, 1024)), pl.BlockSpec((COL, 1024), lambda j: (j, 0))],
        cols(1024),
        jax.ShapeDtypeStruct((1024, 1024), BF),
        [],
        int(2.15e9),
        6 << 20,
        24,
        "project_back",
    )(d_edge, w_out)


def atom_sums_body(d_preact, src, dst, sums, scatter):
    @pl.when(pl.program_id(0) == 0)
    def _():
        fill_scatter(scatter.at[pl.ds(0, 1024)], src[...])
        fill_scatter(scatter.at[pl.ds(1024, 1024)], dst[...])

    sums[...] = dot_nn(scatter[...], d_preact[...]).astype(BF)


def atom_sums(d_preact, src, dst):
    return call(
        atom_sums_body,
        (STEPS,),
        [cols(1024), full((1, 1024)), full((1, 1024))],
        cols(2048),
        jax.ShapeDtypeStruct((2048, 1024), BF),
        [pltpu.VMEM((2048, 1024), BF)],
        int(2.15e9 * 2),
        6 << 20,
        28,
        "atom_sums",
    )(d_preact, src, dst)


def atom_backward_body(sums, w_src, w_dst, keep, give):
    back = dot_nt(sums[:1024], w_src[...]) + dot_nt(sums[1024:], w_dst[...])
    keep[...] = back[:512].astype(BF)
    give[...] = back[512:].astype(BF)


def atom_backward(sums, w_pair):
    return call(
        atom_backward_body,
        (STEPS,),
        [
            full((2048, 1024)),
            pl.BlockSpec((COL, 1024), lambda j: (j, 0)),
            pl.BlockSpec((COL, 1024), lambda j: (STEPS + j, 0)),
        ],
        [cols(512)] * 2,
        [jax.ShapeDtypeStruct((512, 1024), BF)] * 2,
        [],
        int(2.15e9 * 2),
        10 << 20,
        26,
        "atom_backward",
    )(sums, w_pair, w_pair)


def swap_core(x):
    return lax.ppermute(x, "graph", [(i, i ^ 1) for i in range(8)])


def along_z(x, shift):
    return lax.ppermute(
        x, "graph", [(2 * z + c, 2 * ((z + shift) % 4) + c) for z in range(4) for c in range(2)]
    )


def gather_graph(x, beside=None):
    same = [along_z(x, -k) for k in (1, 2, 3)]
    if beside is not None:
        *same, beside = tie(*same, beside())
    same = [x] + same
    blocks = same + [swap_core(block) for block in same]
    return blocks, beside


def scatter_graph(keep, give):
    both = (keep.astype(F32) + swap_core(give).astype(F32)).astype(BF).reshape(4, 128, -1)
    return [both[0]] + [along_z(both[k], k) for k in (1, 2, 3)]


def add_core(keep, give):
    return keep + swap_core(give)


def spread_chunks(both):
    groups = [[i for i in range(128) if i % 2 == c] for c in range(2)]
    return lax.all_to_all(both, ("dp", "graph"), 0, 0, tiled=True, axis_index_groups=groups)


def add_chunks(spread):
    return jnp.sum(spread.astype(F32), axis=0)


def tie(*values):
    return lax.optimization_barrier(values)


def on_device(
    atom_embed,
    edge_embed,
    source,
    target,
    trip_source,
    trip_target,
    trip_count,
    basis_values,
    w_pair,
    w_basis,
    w_out,
    w_atom,
    atom_cotan,
    edge_cotan,
):
    place = lax.axis_index("graph")
    chip, core = place // 2, place % 2

    def local(index):
        owner = index // 128
        step = (owner // 2 - chip) & 3
        return (((owner & 1) ^ core) * 4 + step) * 128 + (index & 127)

    own_atoms, cotan = atom_embed[0], atom_cotan[0]
    src, dst = local(source), local(target)
    slot = lax.broadcasted_iota(jnp.int32, trip_target.shape, 1)
    tin, ttg = trip_source, jnp.where(slot < trip_count, trip_target, -1)
    basis = basis_values[0]

    blocks, (filters, turned) = gather_graph(own_atoms, lambda: prepare(basis, w_basis))
    rows, in_rows, slope, summed, new_edges, keep, give = forward(
        blocks, src, dst, tin, ttg, w_pair, filters, edge_embed[0], w_out
    )
    atom_sum, new_atoms, d_z, d_sum = atom_update(
        scatter_graph(keep, give), own_atoms, cotan, w_atom
    )
    d_edge, keep, give = edge_backward(
        gather_graph(d_sum)[0], core[None], dst, edge_cotan[0], summed, atom_sum, d_z
    )
    both = add_core(keep, give)
    d_summed, both = tie(project_back(d_edge, w_out), both)
    spread = spread_chunks(both)
    d_preact, keep, give = trip_backward(
        core[None], d_summed, in_rows, slope, turned, filters, rows, tin, ttg
    )
    d_preact, spread, keep, give = tie(d_preact, spread, keep, give)
    out_atom = add_chunks(spread)
    both = add_core(keep, give)
    sums, both, out_atom = tie(atom_sums(d_preact, src, dst), both, out_atom)
    spread = spread_chunks(both)
    back = scatter_graph(*atom_backward(sums, w_pair))
    grads_new = (cotan.astype(F32) + sum(b.astype(F32) for b in back)).astype(BF)
    pair = add_chunks(spread)
    pair_total, basis_total = pair[:, :1024], pair[:8, 1024:].reshape(1, 1024)
    out_total, atom_w_total = out_atom[:8], out_atom[8:]
    return (
        new_atoms[None],
        new_edges[None],
        grads_new[None],
        d_edge[None],
        pair_total,
        basis_total,
        out_total,
        atom_w_total,
    )


def solution(mesh):
    rows, flat = P("dp", "graph", None), P("dp", "graph")
    placed = (rows, rows, flat, flat, flat, flat, flat, rows, P(), P(), P(), P(), rows, rows)
    spread = P(("dp", "graph"), None)
    return jax.shard_map(
        on_device,
        mesh=mesh,
        in_specs=placed,
        out_specs=(rows,) * 4 + (spread,) * 4,
        check_vma=False,
    )
```

```python
import jax
import jax.numpy as jnp
from jax import lax
from jax.experimental import pallas as pl
from jax.experimental.pallas import tpu as pltpu
from jax.sharding import PartitionSpec as P

SCALE = 8.0 ** (-0.5)
BF = jnp.bfloat16
F32 = jnp.float32
COL = 512


def dot_nn(a, b):
    return lax.dot_general(a, b, (((1,), (0,)), ((), ())), preferred_element_type=F32)


def dot_nt(a, b):
    return lax.dot_general(a, b, (((1,), (1,)), ((), ())), preferred_element_type=F32)


def dot_tn(a, b):
    return lax.dot_general(a, b, (((0,), (0,)), ((), ())), preferred_element_type=F32)


def silu_slope(value):
    sigma = jax.nn.sigmoid(value)
    return sigma * (1.0 + value * (1.0 - sigma))


def fill_gather(ref, index, at=0):
    length, width = index.shape[1], 1024
    column = jnp.broadcast_to(index, (128, length)).T
    lane = lax.broadcasted_iota(jnp.int32, (length, 128), 1)
    for b in range(width // 128):
        hit = jnp.where(column == lane + b * 128, 1.0, 0.0).astype(BF)
        ref[:, at + b * 128 : at + (b + 1) * 128] = hit


def fill_scatter(ref, index):
    length, width = index.shape[1], 1024
    sub = lax.broadcasted_iota(jnp.int32, (128, length), 0)
    for b in range(width // 128):
        hit = jnp.where(sub + b * 128 == index, 1.0, 0.0).astype(BF)
        ref[b * 128 : (b + 1) * 128, :] = hit


def full(shape):
    return pl.BlockSpec(shape, lambda j: (0,) * len(shape))


def cols(rows, width=COL):
    return pl.BlockSpec((rows, width), lambda j: (0, j))


def call(body, grid, in_specs, out_specs, out_shape, scratch, flops, moved, mib, name):
    return pl.pallas_call(
        body,
        grid=grid,
        in_specs=in_specs,
        out_specs=out_specs,
        out_shape=out_shape,
        scratch_shapes=scratch,
        compiler_params=pltpu.CompilerParams(vmem_limit_bytes=mib << 20),
        cost_estimate=pl.CostEstimate(flops=flops, bytes_accessed=moved, transcendentals=0),
        name=name,
    )


STEPS = 1024 // COL


def early(rows, width=COL):
    return pl.BlockSpec((rows, width), lambda j: (0, jnp.minimum(j, STEPS - 1)))


def late(rows, width=COL):
    return pl.BlockSpec((rows, width), lambda j: (0, jnp.maximum(j - STEPS, 0)))


def prepare_body(basis, w_basis, filters, turned):
    filters[...] = dot_nn(basis[...], w_basis[...]).astype(BF)

    @pl.when(pl.program_id(0) == 0)
    def _():
        turned[...] = basis[...].T


def prepare(basis, w_basis):
    return call(
        prepare_body,
        (STEPS,),
        [full((2048, 128)), cols(128)],
        [cols(2048), full((128, 2048))],
        [jax.ShapeDtypeStruct((2048, 1024), BF), jax.ShapeDtypeStruct((128, 2048), BF)],
        [],
        int(2.15e9 * 0.6),
        6 << 20,
        60,
        "prepare",
    )(basis, w_basis)


def forward_body(*refs):
    blocks = refs[:8]
    src, dst, tin, ttg, w_pair, filters, edge, w_out = refs[8:16]
    rows_out, in_rows, slope, summed_out, new_edges, keep, give = refs[16:23]
    atoms, one_hot, gather_in, scatter_tgt, msg, rows, summed, sems = refs[23:]
    rows_copy = pltpu.make_async_copy(rows, rows_out, sems.at[0])
    summed_copy = pltpu.make_async_copy(summed, summed_out, sems.at[1])
    step = pl.program_id(0)

    @pl.when(step == 0)
    def _():
        for b in range(8):
            atoms[b * 128 : (b + 1) * 128, :] = blocks[b][...]
        for part, index in enumerate((src, dst)):
            fill_gather(one_hot, index[...])
            rows[:, part * 1024 : (part + 1) * 1024] = dot_nn(one_hot[...], atoms[...]).astype(BF)
        rows_copy.start()
        fill_gather(gather_in, tin[...])
        fill_scatter(scatter_tgt, ttg[...])

    @pl.when(step < STEPS)
    def _():
        preact = dot_nn(rows[...], w_pair[...])
        sigma = jax.nn.sigmoid(preact)
        slope[...] = (sigma * (1.0 + preact * (1.0 - sigma))).astype(BF)
        activated = (preact * sigma).astype(BF)
        for t in range(2):
            part = slice(t * 1024, (t + 1) * 1024)
            found = dot_nn(gather_in[part, :], activated).astype(BF)
            in_rows[part, :] = found
            msg[part, :] = found * filters[part, :]
        at = pl.ds(pl.multiple_of(step * COL, COL), COL)
        summed[:, at] = dot_nn(scatter_tgt[...], msg[...]).astype(BF)

    @pl.when(step == STEPS)
    def _():
        summed_copy.start()
        fill_scatter(one_hot, dst[...])

    @pl.when(step >= STEPS)
    def _():
        new = (edge[...].astype(F32) + dot_nn(summed[...], w_out[...])).astype(BF)
        new_edges[...] = new
        total = dot_nn(one_hot[...], new).astype(BF)
        keep[...] = total[:512]
        give[...] = total[512:]

    @pl.when(step == 2 * STEPS - 1)
    def _():
        rows_copy.wait()
        summed_copy.wait()


def forward(blocks, src, dst, tin, ttg, w_pair, filters, edge, w_out):
    return call(
        forward_body,
        (2 * STEPS,),
        [full((128, 1024))] * 8
        + [full((1, 1024))] * 2
        + [full((1, 2048))] * 2
        + [early(2048), early(2048), late(1024), late(1024)],
        [pl.BlockSpec(memory_space=pl.ANY), early(2048), early(1024), pl.BlockSpec(memory_space=pl.ANY)]
        + [late(1024), late(512), late(512)],
        [
            jax.ShapeDtypeStruct((1024, 2048), BF),
            jax.ShapeDtypeStruct((2048, 1024), BF),
            jax.ShapeDtypeStruct((1024, 1024), BF),
            jax.ShapeDtypeStruct((1024, 1024), BF),
            jax.ShapeDtypeStruct((1024, 1024), BF),
            jax.ShapeDtypeStruct((512, 1024), BF),
            jax.ShapeDtypeStruct((512, 1024), BF),
        ],
        [
            pltpu.VMEM((1024, 1024), BF),
            pltpu.VMEM((1024, 1024), BF),
            pltpu.VMEM((2048, 1024), BF),
            pltpu.VMEM((1024, 2048), BF),
            pltpu.VMEM((2048, COL), BF),
            pltpu.VMEM((1024, 2048), BF),
            pltpu.VMEM((1024, 1024), BF),
            pltpu.SemaphoreType.DMA((2,)),
        ],
        int(2.15e9 * 10.3),
        28 << 20,
        60,
        "forward",
    )(*blocks, src, dst, tin, ttg, w_pair, filters, edge, w_out)


def atom_body(y0, y1, y2, y3, atoms, cotan, w_atom, atom_sum, new_atoms, d_z, d_sum):
    total = y0[...].astype(F32) + y1[...].astype(F32) + y2[...].astype(F32) + y3[...].astype(F32)
    held = (total * SCALE).astype(BF)
    atom_sum[...] = held
    z = dot_nn(held, w_atom[...])
    sigma = jax.nn.sigmoid(z)
    new_atoms[...] = (atoms[...].astype(F32) + z * sigma).astype(BF)
    dz = (cotan[...].astype(F32) * (sigma * (1.0 + z * (1.0 - sigma)))).astype(BF)
    d_z[...] = dz
    d_sum[...] = dot_nt(dz, w_atom[...]).astype(BF)


def atom_update(ys, atoms, cotan, w_atom):
    return call(
        atom_body,
        (1,),
        [full((128, 1024))] * 6 + [full((1024, 1024))],
        [full((128, 1024))] * 4,
        [jax.ShapeDtypeStruct((128, 1024), BF)] * 4,
        [],
        int(2.15e9 / 4),
        5 << 20,
        14,
        "atom_update",
    )(*ys, atoms, cotan, w_atom)


def own_rows(core, even, odd, keep, give):
    even, odd = even.astype(BF), odd.astype(BF)
    keep[...] = jnp.where(core == 0, even, odd)
    give[...] = jnp.where(core == 0, odd, even)


SCALAR = pl.BlockSpec(memory_space=pltpu.SMEM)


def back_edge_body(*refs):
    blocks = refs[:8]
    core, dst, cotan, summed, atom_sum, d_z = refs[8:14]
    d_edge, keep, give = refs[14:17]
    found, gather_dst = refs[17:]

    @pl.when(pl.program_id(0) == 0)
    def _():
        fill_gather(gather_dst, dst[...])

    for b in range(8):
        found[b * 128 : (b + 1) * 128, :] = blocks[b][...]
    back = (cotan[...].astype(F32) + SCALE * dot_nn(gather_dst[...], found[...])).astype(BF)
    d_edge[...] = back
    out = dot_tn(summed[...], back).reshape(64, 2, 8, COL)
    atom = dot_tn(atom_sum[...], d_z[...]).reshape(64, 2, 8, COL)
    both = jnp.concatenate([out, atom], axis=2)
    own_rows(core[0], both[:, 0], both[:, 1], keep, give)


def edge_backward(blocks, core, dst, cotan, summed, atom_sum, d_z):
    chunks = pl.BlockSpec((64, 16, COL), lambda j: (0, 0, j))
    return call(
        back_edge_body,
        (STEPS,),
        [cols(128)] * 8
        + [SCALAR, full((1, 1024)), cols(1024), full((1024, 1024))]
        + [full((128, 1024)), cols(128)],
        [cols(1024), chunks, chunks],
        [
            jax.ShapeDtypeStruct((1024, 1024), BF),
            jax.ShapeDtypeStruct((64, 16, 1024), BF),
            jax.ShapeDtypeStruct((64, 16, 1024), BF),
        ],
        [pltpu.VMEM((1024, COL), BF), pltpu.VMEM((1024, 1024), BF)],
        int(2.15e9 * 2.2),
        12 << 20,
        40,
        "edge_backward",
    )(*blocks, core, dst, cotan, summed, atom_sum, d_z)


CHUNK = 1024 + 128
FOLD = 1024 // STEPS
PART = 2048 // STEPS


def trip_body(*refs):
    core, d_summed, in_rows, slope, turned, filters, rows, tin, ttg, src, dst = refs[:11]
    sums, keep, give = refs[11:14]
    one_hot, scatter_in, msg, d_filter, held, grad_basis, folded = refs[14:]
    step = pl.program_id(0)

    @pl.when(step == 0)
    def _():
        fill_gather(one_hot, ttg[...])
        fill_scatter(scatter_in, tin[...])

    @pl.when(step < STEPS)
    def _():
        for t in range(2):
            part = slice(t * 1024, (t + 1) * 1024)
            d_trip = dot_nn(one_hot[part, :], d_summed[...]).astype(BF)
            d_filter[part, :] = d_trip * in_rows[part, :]
            msg[part, :] = d_trip * filters[part, :]
        at = pl.ds(pl.multiple_of(step * COL, COL), COL)
        grad_basis[:, at] = dot_nn(turned[...], d_filter[...])
        d_active = dot_nn(scatter_in[...], msg[...])
        held[:, at] = (d_active * slope[...].astype(F32)).astype(BF)

    @pl.when(step == STEPS)
    def _():
        fill_scatter(one_hot.at[pl.ds(0, 1024)], src[...])
        fill_scatter(one_hot.at[pl.ds(1024, 1024)], dst[...])
        for i in range(8):
            folded[pl.ds(i, 128, stride=8), :] = grad_basis[:, i * 128 : (i + 1) * 128]

    @pl.when(step >= STEPS)
    def _():
        both = dot_tn(rows[...], held[...]).reshape(64 // STEPS, 2, 16, 1024)
        at = pl.ds(pl.multiple_of((step - STEPS) * FOLD, FOLD), FOLD)
        fold = folded[at, :].reshape(64 // STEPS, 2, 8, 128)
        fold = jnp.concatenate([fold, jnp.zeros_like(fold)], axis=2)
        both = jnp.concatenate([both, fold], axis=3)
        own_rows(core[0], both[:, 0], both[:, 1], keep, give)
        at = pl.ds(pl.multiple_of((step - STEPS) * PART, PART), PART)
        sums[...] = dot_nn(one_hot[at, :], held[...]).astype(BF)


def own_rows(core, even, odd, keep, give):
    even, odd = even.astype(BF), odd.astype(BF)
    keep[...] = jnp.where(core == 0, even, odd)
    give[...] = jnp.where(core == 0, odd, even)


def trip_backward(core, d_summed, in_rows, slope, turned, filters, rows, tin, ttg, src, dst):
    chunks = pl.BlockSpec((64 // STEPS, 16, CHUNK), lambda j: (jnp.maximum(j - STEPS, 0), 0, 0))
    return call(
        trip_body,
        (2 * STEPS,),
        [
            SCALAR,
            early(1024),
            early(2048),
            early(1024),
            full((128, 2048)),
            early(2048),
            late(1024, 2048 // STEPS),
            full((1, 2048)),
            full((1, 2048)),
            full((1, 1024)),
            full((1, 1024)),
        ],
        [pl.BlockSpec((PART, 1024), lambda j: (jnp.maximum(j - STEPS, 0), 0)), chunks, chunks],
        [
            jax.ShapeDtypeStruct((2048, 1024), BF),
            jax.ShapeDtypeStruct((64, 16, CHUNK), BF),
            jax.ShapeDtypeStruct((64, 16, CHUNK), BF),
        ],
        [
            pltpu.VMEM((2048, 1024), BF),
            pltpu.VMEM((1024, 2048), BF),
            pltpu.VMEM((2048, COL), BF),
            pltpu.VMEM((2048, COL), BF),
            pltpu.VMEM((1024, 1024), BF),
            pltpu.VMEM((128, 1024), F32),
            pltpu.VMEM((1024, 128), F32),
        ],
        int(2.15e9 * 8.6),
        24 << 20,
        60,
        "trip_backward",
    )(core, d_summed, in_rows, slope, turned, filters, rows, tin, ttg, src, dst)


def project_body(d_edge, w_out, d_summed):
    d_summed[...] = dot_nt(d_edge[...], w_out[...]).astype(BF)


def project_back(d_edge, w_out):
    return call(
        project_body,
        (STEPS,),
        [full((1024, 1024)), pl.BlockSpec((COL, 1024), lambda j: (j, 0))],
        cols(1024),
        jax.ShapeDtypeStruct((1024, 1024), BF),
        [],
        int(2.15e9),
        6 << 20,
        24,
        "project_back",
    )(d_edge, w_out)


def atom_backward_body(sums, w_src, w_dst, keep, give):
    back = dot_nt(sums[:1024], w_src[...]) + dot_nt(sums[1024:], w_dst[...])
    keep[...] = back[:512].astype(BF)
    give[...] = back[512:].astype(BF)


def atom_backward(sums, w_pair):
    return call(
        atom_backward_body,
        (STEPS,),
        [
            full((2048, 1024)),
            pl.BlockSpec((COL, 1024), lambda j: (j, 0)),
            pl.BlockSpec((COL, 1024), lambda j: (STEPS + j, 0)),
        ],
        [cols(512)] * 2,
        [jax.ShapeDtypeStruct((512, 1024), BF)] * 2,
        [],
        int(2.15e9 * 2),
        10 << 20,
        60,
        "atom_backward",
    )(sums, w_pair, w_pair)


def swap_core(x):
    return lax.ppermute(x, "graph", [(i, i ^ 1) for i in range(8)])


def along_z(x, shift):
    return lax.ppermute(
        x, "graph", [(2 * z + c, 2 * ((z + shift) % 4) + c) for z in range(4) for c in range(2)]
    )


def gather_graph(x, beside=None):
    same = [along_z(x, -k) for k in (1, 2, 3)]
    if beside is not None:
        *same, beside = tie(*same, beside())
    same = [x] + same
    blocks = same + [swap_core(block) for block in same]
    return blocks, beside


def scatter_graph(keep, give):
    both = (keep.astype(F32) + swap_core(give).astype(F32)).astype(BF).reshape(4, 128, -1)
    return [both[0]] + [along_z(both[k], k) for k in (1, 2, 3)]


def add_core(keep, give):
    return keep + swap_core(give)


def spread_chunks(both):
    groups = [[i for i in range(128) if i % 2 == c] for c in range(2)]
    return lax.all_to_all(both, ("dp", "graph"), 0, 0, tiled=True, axis_index_groups=groups)


def add_chunks(spread):
    return jnp.sum(spread.astype(F32), axis=0)


def spread_plane(both):
    return lax.all_to_all(both, "dp", 0, 0, tiled=True)


def add_plane(spread):
    return jnp.sum(spread.reshape(16, 4, 16, -1).astype(F32), axis=0).astype(BF)


def add_line(plane):
    groups = [[2 * z + c for z in range(4)] for c in range(2)]
    last = lax.all_to_all(plane, "graph", 0, 0, tiled=True, axis_index_groups=groups)
    return jnp.sum(last.astype(F32), axis=0)


def tie(*values):
    return lax.optimization_barrier(values)


def on_device(
    atom_embed,
    edge_embed,
    source,
    target,
    trip_source,
    trip_target,
    trip_count,
    basis_values,
    w_pair,
    w_basis,
    w_out,
    w_atom,
    atom_cotan,
    edge_cotan,
):
    place = lax.axis_index("graph")
    chip, core = place // 2, place % 2

    def local(index):
        owner = index // 128
        step = (owner // 2 - chip) & 3
        return (((owner & 1) ^ core) * 4 + step) * 128 + (index & 127)

    own_atoms, cotan = atom_embed[0], atom_cotan[0]
    src, dst = local(source), local(target)
    slot = lax.broadcasted_iota(jnp.int32, trip_target.shape, 1)
    tin, ttg = trip_source, jnp.where(slot < trip_count, trip_target, -1)
    basis = basis_values[0]

    blocks, (filters, turned) = gather_graph(own_atoms, lambda: prepare(basis, w_basis))
    rows, in_rows, slope, summed, new_edges, keep, give = forward(
        blocks, src, dst, tin, ttg, w_pair, filters, edge_embed[0], w_out
    )
    atom_sum, new_atoms, d_z, d_sum = atom_update(
        scatter_graph(keep, give), own_atoms, cotan, w_atom
    )
    d_edge, keep, give = edge_backward(
        gather_graph(d_sum)[0], core[None], dst, edge_cotan[0], summed, atom_sum, d_z
    )
    both = add_core(keep, give)
    d_summed, both = tie(project_back(d_edge, w_out), both)
    spread = spread_chunks(both)
    sums, keep, give = trip_backward(
        core[None], d_summed, in_rows, slope, turned, filters, rows, tin, ttg, src, dst
    )
    sums, spread, keep, give = tie(sums, spread, keep, give)
    out_atom = add_chunks(spread)
    both = add_core(keep, give)
    sums, both, out_atom = tie(sums, both, out_atom)
    spread = spread_plane(both)
    back = scatter_graph(*atom_backward(sums, w_pair))
    grads_new = (cotan.astype(F32) + sum(b.astype(F32) for b in back)).astype(BF)
    pair = add_line(add_plane(spread))
    pair_total, basis_total = pair[:, :1024], pair[:8, 1024:].reshape(1, 1024)
    out_total, atom_w_total = out_atom[:8], out_atom[8:]
    return (
        new_atoms[None],
        new_edges[None],
        grads_new[None],
        d_edge[None],
        pair_total,
        basis_total,
        out_total,
        atom_w_total,
    )


def solution(mesh):
    rows, flat = P("dp", "graph", None), P("dp", "graph")
    placed = (rows, rows, flat, flat, flat, flat, flat, rows, P(), P(), P(), P(), rows, rows)
    spread = P(("dp", "graph"), None)
    return jax.shard_map(
        on_device,
        mesh=mesh,
        in_specs=placed,
        out_specs=(rows,) * 4 + (spread,) * 4,
        check_vma=False,
    )
```

```python
import jax
import jax.numpy as jnp
from jax import lax
from jax.experimental import pallas as pl
from jax.experimental.pallas import tpu as pltpu
from jax.sharding import PartitionSpec as P

SCALE = 8.0 ** (-0.5)
BF = jnp.bfloat16
F32 = jnp.float32
COL = 512


def dot_nn(a, b):
    return lax.dot_general(a, b, (((1,), (0,)), ((), ())), preferred_element_type=F32)


def dot_nt(a, b):
    return lax.dot_general(a, b, (((1,), (1,)), ((), ())), preferred_element_type=F32)


def dot_tn(a, b):
    return lax.dot_general(a, b, (((0,), (0,)), ((), ())), preferred_element_type=F32)


def silu_slope(value):
    sigma = jax.nn.sigmoid(value)
    return sigma * (1.0 + value * (1.0 - sigma))


def fill_gather(ref, index, at=0):
    length, width = index.shape[1], 1024
    column = jnp.broadcast_to(index, (128, length)).T
    lane = lax.broadcasted_iota(jnp.int32, (length, 128), 1)
    for b in range(width // 128):
        hit = jnp.where(column == lane + b * 128, 1.0, 0.0).astype(BF)
        ref[:, at + b * 128 : at + (b + 1) * 128] = hit


def fill_scatter(ref, index):
    length, width = index.shape[1], 1024
    sub = lax.broadcasted_iota(jnp.int32, (128, length), 0)
    for b in range(width // 128):
        hit = jnp.where(sub + b * 128 == index, 1.0, 0.0).astype(BF)
        ref[b * 128 : (b + 1) * 128, :] = hit


def full(shape):
    return pl.BlockSpec(shape, lambda j: (0,) * len(shape))


def cols(rows, width=COL):
    return pl.BlockSpec((rows, width), lambda j: (0, j))


def call(body, grid, in_specs, out_specs, out_shape, scratch, flops, moved, mib, name):
    return pl.pallas_call(
        body,
        grid=grid,
        in_specs=in_specs,
        out_specs=out_specs,
        out_shape=out_shape,
        scratch_shapes=scratch,
        compiler_params=pltpu.CompilerParams(vmem_limit_bytes=mib << 20),
        cost_estimate=pl.CostEstimate(flops=flops, bytes_accessed=moved, transcendentals=0),
        name=name,
    )


STEPS = 1024 // COL


def early(rows, width=COL):
    return pl.BlockSpec((rows, width), lambda j: (0, jnp.minimum(j, STEPS - 1)))


def late(rows, width=COL):
    return pl.BlockSpec((rows, width), lambda j: (0, jnp.maximum(j - STEPS, 0)))


def prepare_body(basis, w_basis, filters, turned):
    filters[...] = dot_nn(basis[...], w_basis[...]).astype(BF)

    @pl.when(pl.program_id(0) == 0)
    def _():
        turned[...] = basis[...].T


def prepare(basis, w_basis):
    return call(
        prepare_body,
        (STEPS,),
        [full((2048, 128)), cols(128)],
        [cols(2048), full((128, 2048))],
        [jax.ShapeDtypeStruct((2048, 1024), BF), jax.ShapeDtypeStruct((128, 2048), BF)],
        [],
        int(2.15e9 * 0.6),
        6 << 20,
        60,
        "prepare",
    )(basis, w_basis)


def forward_body(*refs):
    blocks = refs[:8]
    src, dst, tin, ttg, w_pair, filters, edge, w_out = refs[8:16]
    rows_out, in_rows, slope, summed_out, new_edges, keep, give = refs[16:23]
    atoms, one_hot, gather_in, scatter_tgt, msg, rows, summed, sems = refs[23:]
    rows_copy = pltpu.make_async_copy(rows, rows_out, sems.at[0])
    summed_copy = pltpu.make_async_copy(summed, summed_out, sems.at[1])
    step = pl.program_id(0)

    @pl.when(step == 0)
    def _():
        for b in range(8):
            atoms[b * 128 : (b + 1) * 128, :] = blocks[b][...]
        for part, index in enumerate((src, dst)):
            fill_gather(one_hot, index[...])
            rows[:, part * 1024 : (part + 1) * 1024] = dot_nn(one_hot[...], atoms[...]).astype(BF)
        rows_copy.start()
        fill_gather(gather_in, tin[...])
        fill_scatter(scatter_tgt, ttg[...])

    @pl.when(step < STEPS)
    def _():
        preact = dot_nn(rows[...], w_pair[...])
        sigma = jax.nn.sigmoid(preact)
        slope[...] = (sigma * (1.0 + preact * (1.0 - sigma))).astype(BF)
        activated = (preact * sigma).astype(BF)
        for t in range(2):
            part = slice(t * 1024, (t + 1) * 1024)
            found = dot_nn(gather_in[part, :], activated).astype(BF)
            in_rows[part, :] = found
            msg[part, :] = found * filters[part, :]
        at = pl.ds(pl.multiple_of(step * COL, COL), COL)
        summed[:, at] = dot_nn(scatter_tgt[...], msg[...]).astype(BF)

    @pl.when(step == STEPS)
    def _():
        summed_copy.start()
        fill_scatter(one_hot, dst[...])

    @pl.when(step >= STEPS)
    def _():
        new = (edge[...].astype(F32) + dot_nn(summed[...], w_out[...])).astype(BF)
        new_edges[...] = new
        total = dot_nn(one_hot[...], new).astype(BF)
        keep[...] = total[:512]
        give[...] = total[512:]

    @pl.when(step == 2 * STEPS - 1)
    def _():
        rows_copy.wait()
        summed_copy.wait()


def forward(blocks, src, dst, tin, ttg, w_pair, filters, edge, w_out):
    return call(
        forward_body,
        (2 * STEPS,),
        [full((128, 1024))] * 8
        + [full((1, 1024))] * 2
        + [full((1, 2048))] * 2
        + [early(2048), early(2048), late(1024), late(1024)],
        [pl.BlockSpec(memory_space=pl.ANY), early(2048), early(1024), pl.BlockSpec(memory_space=pl.ANY)]
        + [late(1024), late(512), late(512)],
        [
            jax.ShapeDtypeStruct((1024, 2048), BF),
            jax.ShapeDtypeStruct((2048, 1024), BF),
            jax.ShapeDtypeStruct((1024, 1024), BF),
            jax.ShapeDtypeStruct((1024, 1024), BF),
            jax.ShapeDtypeStruct((1024, 1024), BF),
            jax.ShapeDtypeStruct((512, 1024), BF),
            jax.ShapeDtypeStruct((512, 1024), BF),
        ],
        [
            pltpu.VMEM((1024, 1024), BF),
            pltpu.VMEM((1024, 1024), BF),
            pltpu.VMEM((2048, 1024), BF),
            pltpu.VMEM((1024, 2048), BF),
            pltpu.VMEM((2048, COL), BF),
            pltpu.VMEM((1024, 2048), BF),
            pltpu.VMEM((1024, 1024), BF),
            pltpu.SemaphoreType.DMA((2,)),
        ],
        int(2.15e9 * 10.3),
        28 << 20,
        60,
        "forward",
    )(*blocks, src, dst, tin, ttg, w_pair, filters, edge, w_out)


def atom_body(y0, y1, y2, y3, atoms, cotan, w_atom, atom_sum, new_atoms, d_z, d_sum):
    total = y0[...].astype(F32) + y1[...].astype(F32) + y2[...].astype(F32) + y3[...].astype(F32)
    held = (total * SCALE).astype(BF)
    atom_sum[...] = held
    z = dot_nn(held, w_atom[...])
    sigma = jax.nn.sigmoid(z)
    new_atoms[...] = (atoms[...].astype(F32) + z * sigma).astype(BF)
    dz = (cotan[...].astype(F32) * (sigma * (1.0 + z * (1.0 - sigma)))).astype(BF)
    d_z[...] = dz
    d_sum[...] = dot_nt(dz, w_atom[...]).astype(BF)


def atom_update(ys, atoms, cotan, w_atom):
    return call(
        atom_body,
        (1,),
        [full((128, 1024))] * 6 + [full((1024, 1024))],
        [full((128, 1024))] * 4,
        [jax.ShapeDtypeStruct((128, 1024), BF)] * 4,
        [],
        int(2.15e9 / 4),
        5 << 20,
        14,
        "atom_update",
    )(*ys, atoms, cotan, w_atom)


def own_rows(core, even, odd, keep, give):
    even, odd = even.astype(BF), odd.astype(BF)
    keep[...] = jnp.where(core == 0, even, odd)
    give[...] = jnp.where(core == 0, odd, even)


SCALAR = pl.BlockSpec(memory_space=pltpu.SMEM)


def back_edge_body(*refs):
    blocks = refs[:8]
    core, dst, cotan, summed, atom_sum, d_z = refs[8:14]
    d_edge, keep, give = refs[14:17]
    found, gather_dst = refs[17:]

    @pl.when(pl.program_id(0) == 0)
    def _():
        fill_gather(gather_dst, dst[...])

    for b in range(8):
        found[b * 128 : (b + 1) * 128, :] = blocks[b][...]
    back = (cotan[...].astype(F32) + SCALE * dot_nn(gather_dst[...], found[...])).astype(BF)
    d_edge[...] = back
    out = dot_tn(summed[...], back).reshape(64, 2, 8, COL)
    atom = dot_tn(atom_sum[...], d_z[...]).reshape(64, 2, 8, COL)
    both = jnp.concatenate([out, atom], axis=2)
    own_rows(core[0], both[:, 0], both[:, 1], keep, give)


def edge_backward(blocks, core, dst, cotan, summed, atom_sum, d_z):
    chunks = pl.BlockSpec((64, 16, COL), lambda j: (0, 0, j))
    return call(
        back_edge_body,
        (STEPS,),
        [cols(128)] * 8
        + [SCALAR, full((1, 1024)), cols(1024), full((1024, 1024))]
        + [full((128, 1024)), cols(128)],
        [cols(1024), chunks, chunks],
        [
            jax.ShapeDtypeStruct((1024, 1024), BF),
            jax.ShapeDtypeStruct((64, 16, 1024), BF),
            jax.ShapeDtypeStruct((64, 16, 1024), BF),
        ],
        [pltpu.VMEM((1024, COL), BF), pltpu.VMEM((1024, 1024), BF)],
        int(2.15e9 * 2.2),
        12 << 20,
        40,
        "edge_backward",
    )(*blocks, core, dst, cotan, summed, atom_sum, d_z)


CHUNK = 1024 + 128
FOLD = 1024 // STEPS


def trip_body(*refs):
    core, d_edge, w_out, in_rows, slope, turned, filters, rows, tin, ttg = refs[:10]
    d_preact, keep, give = refs[10:13]
    gather_tgt, scatter_in, msg, d_filter, held, grad_basis, folded = refs[13:]
    step = pl.program_id(0)

    @pl.when(step == 0)
    def _():
        fill_gather(gather_tgt, ttg[...])
        fill_scatter(scatter_in, tin[...])

    @pl.when(step < STEPS)
    def _():
        d_summed = dot_nt(d_edge[...], w_out[...]).astype(BF)
        for t in range(2):
            part = slice(t * 1024, (t + 1) * 1024)
            d_trip = dot_nn(gather_tgt[part, :], d_summed).astype(BF)
            d_filter[part, :] = d_trip * in_rows[part, :]
            msg[part, :] = d_trip * filters[part, :]
        at = pl.ds(pl.multiple_of(step * COL, COL), COL)
        grad_basis[:, at] = dot_nn(turned[...], d_filter[...])
        d_active = dot_nn(scatter_in[...], msg[...])
        d_pre = (d_active * slope[...].astype(F32)).astype(BF)
        d_preact[...] = d_pre
        held[:, at] = d_pre

    @pl.when(step == STEPS)
    def _():
        for i in range(8):
            folded[pl.ds(i, 128, stride=8), :] = grad_basis[:, i * 128 : (i + 1) * 128]

    @pl.when(step >= STEPS)
    def _():
        both = dot_tn(rows[...], held[...]).reshape(64 // STEPS, 2, 16, 1024)
        at = pl.ds(pl.multiple_of((step - STEPS) * FOLD, FOLD), FOLD)
        fold = folded[at, :].reshape(64 // STEPS, 2, 8, 128)
        fold = jnp.concatenate([fold, jnp.zeros_like(fold)], axis=2)
        both = jnp.concatenate([both, fold], axis=3)
        own_rows(core[0], both[:, 0], both[:, 1], keep, give)


def own_rows(core, even, odd, keep, give):
    even, odd = even.astype(BF), odd.astype(BF)
    keep[...] = jnp.where(core == 0, even, odd)
    give[...] = jnp.where(core == 0, odd, even)


def trip_backward(core, d_edge, w_out, in_rows, slope, turned, filters, rows, tin, ttg):
    chunks = pl.BlockSpec((64 // STEPS, 16, CHUNK), lambda j: (jnp.maximum(j - STEPS, 0), 0, 0))
    return call(
        trip_body,
        (2 * STEPS,),
        [
            SCALAR,
            full((1024, 1024)),
            pl.BlockSpec((COL, 1024), lambda j: (jnp.minimum(j, STEPS - 1), 0)),
            early(2048),
            early(1024),
            full((128, 2048)),
            early(2048),
            late(1024, 2048 // STEPS),
            full((1, 2048)),
            full((1, 2048)),
        ],
        [early(1024), chunks, chunks],
        [
            jax.ShapeDtypeStruct((1024, 1024), BF),
            jax.ShapeDtypeStruct((64, 16, CHUNK), BF),
            jax.ShapeDtypeStruct((64, 16, CHUNK), BF),
        ],
        [
            pltpu.VMEM((2048, 1024), BF),
            pltpu.VMEM((1024, 2048), BF),
            pltpu.VMEM((2048, COL), BF),
            pltpu.VMEM((2048, COL), BF),
            pltpu.VMEM((1024, 1024), BF),
            pltpu.VMEM((128, 1024), F32),
            pltpu.VMEM((1024, 128), F32),
        ],
        int(2.15e9 * 7.6),
        24 << 20,
        60,
        "trip_backward",
    )(core, d_edge, w_out, in_rows, slope, turned, filters, rows, tin, ttg)


def atom_sums_body(d_preact, src, dst, sums, scatter):
    @pl.when(pl.program_id(0) == 0)
    def _():
        fill_scatter(scatter.at[pl.ds(0, 1024)], src[...])
        fill_scatter(scatter.at[pl.ds(1024, 1024)], dst[...])

    sums[...] = dot_nn(scatter[...], d_preact[...]).astype(BF)


def atom_sums(d_preact, src, dst):
    return call(
        atom_sums_body,
        (STEPS,),
        [cols(1024), full((1, 1024)), full((1, 1024))],
        cols(2048),
        jax.ShapeDtypeStruct((2048, 1024), BF),
        [pltpu.VMEM((2048, 1024), BF)],
        int(2.15e9 * 2),
        6 << 20,
        28,
        "atom_sums",
    )(d_preact, src, dst)


def atom_backward_body(sums, w_src, w_dst, keep, give):
    back = dot_nt(sums[:1024], w_src[...]) + dot_nt(sums[1024:], w_dst[...])
    keep[...] = back[:512].astype(BF)
    give[...] = back[512:].astype(BF)


def atom_backward(sums, w_pair):
    return call(
        atom_backward_body,
        (STEPS,),
        [
            full((2048, 1024)),
            pl.BlockSpec((COL, 1024), lambda j: (j, 0)),
            pl.BlockSpec((COL, 1024), lambda j: (STEPS + j, 0)),
        ],
        [cols(512)] * 2,
        [jax.ShapeDtypeStruct((512, 1024), BF)] * 2,
        [],
        int(2.15e9 * 2),
        10 << 20,
        26,
        "atom_backward",
    )(sums, w_pair, w_pair)


def swap_core(x):
    return lax.ppermute(x, "graph", [(i, i ^ 1) for i in range(8)])


def along_z(x, shift):
    return lax.ppermute(
        x, "graph", [(2 * z + c, 2 * ((z + shift) % 4) + c) for z in range(4) for c in range(2)]
    )


def gather_graph(x, beside=None):
    same = [along_z(x, -k) for k in (1, 2, 3)]
    if beside is not None:
        *same, beside = tie(*same, beside())
    same = [x] + same
    blocks = same + [swap_core(block) for block in same]
    return blocks, beside


def scatter_graph(keep, give):
    both = (keep.astype(F32) + swap_core(give).astype(F32)).astype(BF).reshape(4, 128, -1)
    return [both[0]] + [along_z(both[k], k) for k in (1, 2, 3)]


def add_core(keep, give):
    return keep + swap_core(give)


def spread_chunks(both):
    groups = [[i for i in range(128) if i % 2 == c] for c in range(2)]
    return lax.all_to_all(both, ("dp", "graph"), 0, 0, tiled=True, axis_index_groups=groups)


def add_chunks(spread):
    return jnp.sum(spread.astype(F32), axis=0)


def spread_plane(both):
    return lax.all_to_all(both, "dp", 0, 0, tiled=True)


def add_plane(spread):
    return jnp.sum(spread.reshape(16, 4, 16, -1).astype(F32), axis=0).astype(BF)


def add_line(plane):
    groups = [[2 * z + c for z in range(4)] for c in range(2)]
    last = lax.all_to_all(plane, "graph", 0, 0, tiled=True, axis_index_groups=groups)
    return jnp.sum(last.astype(F32), axis=0)


def tie(*values):
    return lax.optimization_barrier(values)


def on_device(
    atom_embed,
    edge_embed,
    source,
    target,
    trip_source,
    trip_target,
    trip_count,
    basis_values,
    w_pair,
    w_basis,
    w_out,
    w_atom,
    atom_cotan,
    edge_cotan,
):
    place = lax.axis_index("graph")
    chip, core = place // 2, place % 2

    def local(index):
        owner = index // 128
        step = (owner // 2 - chip) & 3
        return (((owner & 1) ^ core) * 4 + step) * 128 + (index & 127)

    own_atoms, cotan = atom_embed[0], atom_cotan[0]
    src, dst = local(source), local(target)
    slot = lax.broadcasted_iota(jnp.int32, trip_target.shape, 1)
    tin, ttg = trip_source, jnp.where(slot < trip_count, trip_target, -1)
    basis = basis_values[0]

    blocks, (filters, turned) = gather_graph(own_atoms, lambda: prepare(basis, w_basis))
    rows, in_rows, slope, summed, new_edges, keep, give = forward(
        blocks, src, dst, tin, ttg, w_pair, filters, edge_embed[0], w_out
    )
    atom_sum, new_atoms, d_z, d_sum = atom_update(
        scatter_graph(keep, give), own_atoms, cotan, w_atom
    )
    d_edge, keep, give = edge_backward(
        gather_graph(d_sum)[0], core[None], dst, edge_cotan[0], summed, atom_sum, d_z
    )
    d_edge, both = tie(d_edge, add_core(keep, give))
    spread = spread_chunks(both)
    d_preact, keep, give = trip_backward(
        core[None], d_edge, w_out, in_rows, slope, turned, filters, rows, tin, ttg
    )
    d_preact, spread, keep, give = tie(d_preact, spread, keep, give)
    out_atom = add_chunks(spread)
    both = add_core(keep, give)
    d_preact, both, out_atom = tie(d_preact, both, out_atom)
    spread = spread_plane(both)
    back = scatter_graph(*atom_backward(atom_sums(d_preact, src, dst), w_pair))
    grads_new = (cotan.astype(F32) + sum(b.astype(F32) for b in back)).astype(BF)
    pair = add_line(add_plane(spread))
    pair_total, basis_total = pair[:, :1024], pair[:8, 1024:].reshape(1, 1024)
    out_total, atom_w_total = out_atom[:8], out_atom[8:]
    return (
        new_atoms[None],
        new_edges[None],
        grads_new[None],
        d_edge[None],
        pair_total,
        basis_total,
        out_total,
        atom_w_total,
    )


def solution(mesh):
    rows, flat = P("dp", "graph", None), P("dp", "graph")
    placed = (rows, rows, flat, flat, flat, flat, flat, rows, P(), P(), P(), P(), rows, rows)
    spread = P(("dp", "graph"), None)
    return jax.shard_map(
        on_device,
        mesh=mesh,
        in_specs=placed,
        out_specs=(rows,) * 4 + (spread,) * 4,
        check_vma=False,
    )
```
